128 devices in a mesh: step: 4 (over y), dp: 32 (over z, x, core).
Axes of the slice: x: 4, y: 4, z: 4, core: 2. Of those that a mesh axis runs over, the one named last changes fastest.
Arguments:
- hidden_rows: bfloat16 [20480, 4096], P(('dp', 'step')), may hold values from -24 to 24
- codes: int32 [20480, 4], P('dp', 'step'), may hold values from 0 to 2047
- targets: int32 [20480, 4], P('dp', 'step'), may hold values from 0 to 2047
- loss_weights: float32 [20480, 4], P('dp', 'step'), may hold values from 8 to 128
- w_in: bfloat16 [4, 4096, 1024], P('step'), may hold values from -0.09375 to 0.09375
- embed: bfloat16 [4, 2048, 1024], P('step'), may hold values from -6 to 6
- w_out: bfloat16 [4, 2048, 1024], P('step'), may hold values from -10 to 10
- gain: bfloat16 [4, 1024], P('step'), may hold values from 0.5 to 1.5
Outputs:
- grad_rows: bfloat16 [20480, 4096], P(('dp', 'step'))
- upd_in: float32 [4, 4096, 1024], P('step', 'dp')
- upd_embed: float32 [4, 2048, 1024], P('step', 'dp')
- upd_out: float32 [4, 2048, 1024], P('step', 'dp')
- upd_gain: float32 [4, 1024], P('step', 'dp')
The draws below stay inside these ranges and needn't reach their ends.
All inputs are finite; a program needn't handle non-finite values.
Results may differ from the reference program's by a relative error of at most 0.035.
Values may be sent and summed in bfloat16 or wider, within the bound.
No kernel may reach another device: no remote copies, remote signals or barrier semaphores. Data moves between devices by JAX's collectives and lax.ppermute only.
A program may use at most 128 MiB of HBM per device.

```python
import math
import jax
import jax.numpy as jnp
import numpy as np
from jax import lax

D = 1024
DT = 4096
CB = 2048
STEPS = 4
FRAMES = 20480


def draw_w_out(key, part):
    key = jax.random.fold_in(key, 7)
    base = jax.random.truncated_normal(key, -4.0, 4.0, (STEPS, CB, D), jnp.float32) * D ** (-0.5)
    return base.astype(jnp.bfloat16)


def touch_ends(result, stream_key, low, high):
    longest = result.shape.index(max(result.shape))
    spots = []
    for shift in (0, 1):
        where = [jax.random.randint(jax.random.fold_in(stream_key, axis), (), 0, length) for axis, length in enumerate(result.shape)]
        where[longest] = (where[longest] + shift) % result.shape[longest]
        spots.append(tuple(where))
    return result.at[spots[0]].set(low).at[spots[1]].set(high)


def strengthened(drawn, key, source, target, shards_of, factor):
    owner, partner = [(jnp.arange(drawn.shape[axis_at]) // (drawn.shape[axis_at] // shards_of)).reshape([-1 if axis == axis_at else 1 for axis in range(drawn.ndim)]) for axis_at in (source, target)]
    chosen = jax.random.permutation(key, shards_of)[partner]
    strong = (owner == chosen) | (owner == (partner + shards_of // 2) % shards_of)
    return jnp.where(strong, factor * drawn, drawn)


def shard_levels(stream_key, dims, split, low, largest):
    level, own = 1.0, jax.random.fold_in(stream_key, 6)
    for position, parts in split:
        heights = jnp.exp(jax.random.uniform(jax.random.fold_in(own, position), (parts,), jnp.float32, low / len(split), largest / len(split)))
        level = level * jnp.repeat(heights, dims[position] // parts).reshape([-1 if axis == position else 1 for axis in range(len(dims))])
    return level


def cumulative_ranks(number_of, skew):
    loads = [(1 << 20) // math.isqrt(grade ** skew) + 1 for grade in range(1, number_of + 1)]
    scale = 1 + sum(loads) // (1 << 30)
    return np.cumsum(np.array([max(1, weight // scale) for weight in loads]))


def ranked(stream_key, extent, count, skew):
    listing = cumulative_ranks(count, skew)
    lot = jax.random.randint(jax.random.fold_in(stream_key, 1), extent, 0, int(listing[count - 1]))
    grade = jnp.searchsorted(jnp.asarray(listing, jnp.int32), lot, side="right")
    return jax.random.permutation(jax.random.fold_in(stream_key, 2), count)[grade].astype(jnp.int32)


def gaussian(stream_key, dims, deviation, bound, shards=(), kind=jnp.bfloat16):
    values = jax.random.normal(stream_key, dims, jnp.float32) * deviation
    if len(shards) > 0:
        values = shard_levels(stream_key, dims, shards, -0.22, 0.18) * values
    return jnp.clip(values, min=-bound, max=bound).astype(kind)


def bell_draw_with(rng, extent, scale, limit, split, heavy, held_as=jnp.bfloat16):
    drawn = scale * jax.random.normal(rng, extent, jnp.float32)
    if split:
        drawn = drawn * shard_levels(rng, extent, split, -0.22, 0.18)
    return jnp.clip(strengthened(drawn, jax.random.fold_in(rng, 3), *heavy), -limit, limit).astype(held_as)


def setup_inputs(seed: int = 0) -> dict:
    keys = jax.random.split(jax.random.key(seed), 9)
    return {
        "hidden_rows": bell_draw_with(keys[0], (FRAMES, DT), 1.0, 24.0, ((0, 128),), (0, 1, 128, 5.5)),
        "codes": touch_ends(ranked(keys[1], (FRAMES, STEPS), CB, 2), jax.random.fold_in(keys[1], 3), 0, CB - 1).astype(jnp.int32),
        "targets": touch_ends(ranked(keys[2], (FRAMES, STEPS), CB, 2), jax.random.fold_in(keys[2], 3), 0, CB - 1).astype(jnp.int32),
        "loss_weights": jnp.clip(jnp.exp(math.log(128.0) - 2.7725887 * jax.random.uniform(keys[3], (FRAMES, STEPS), jnp.float32) ** shard_levels(keys[3], (FRAMES, STEPS), ((0, 32), (1, 4)), -0.2, 0.2)), 8.0, 128.0),
        "w_in": gaussian(keys[4], (STEPS, DT, D), DT ** -0.5, 0.09375, ((0, 4),)),
        "embed": gaussian(keys[5], (STEPS, CB, D), 1.0, 6.0, ((0, 4),)),
        "w_out": draw_w_out(jax.random.fold_in(keys[8], 71), 0),
        "gain": jnp.clip(1.0 + 0.1 * jax.random.normal(keys[7], (STEPS, D), jnp.float32), 0.5, 1.5).astype(jnp.bfloat16),
    }


def normalize(grad):
    return grad * lax.rsqrt(jnp.mean(grad * grad) + 1e-06)

def reference(hidden_rows, codes, targets, loss_weights, w_in, embed, w_out, gain):
    vocab = jnp.arange(CB, dtype=jnp.int32)
    grad_total = jnp.zeros((FRAMES, DT), jnp.float32)
    ins, embs, outs, gains = ([], [], [], [])
    for step_id in range(STEPS):
        weight_in = w_in[step_id]
        head = w_out[step_id]
        scale_gain = gain[step_id].astype(jnp.float32)
        inputs = jnp.dot(hidden_rows, weight_in, preferred_element_type=jnp.float32)
        inputs = inputs + jnp.take(embed[step_id], codes[:, step_id], axis=0).astype(jnp.float32)
        inverse = lax.rsqrt(lax.optimization_barrier(jnp.mean(inputs * inputs, axis=-1, keepdims=True)) + 1e-05)
        normed = (inputs * inverse * scale_gain).astype(jnp.bfloat16)
        logits = jnp.dot(normed, head.T, preferred_element_type=jnp.float32)
        probs = jax.nn.softmax(logits, axis=-1)
        target_hot = (targets[:, step_id][:, None] == vocab[None, :]).astype(jnp.float32)
        dlogits = (loss_weights[:, step_id:step_id + 1] * (probs - target_hot)).astype(jnp.bfloat16)
        dnormed = jnp.dot(dlogits, head, preferred_element_type=jnp.float32)
        gain_grad = lax.optimization_barrier(jnp.sum(dnormed * inputs * inverse, axis=0))
        upstream = dnormed * scale_gain
        dinputs = inverse * upstream - inputs * inverse ** 3 * lax.optimization_barrier(jnp.mean(upstream * inputs, axis=-1, keepdims=True))
        dinputs = dinputs.astype(jnp.bfloat16)
        term = jnp.dot(dinputs, weight_in.T, preferred_element_type=jnp.float32).astype(jnp.bfloat16)
        term = lax.optimization_barrier(term)
        grad_total = grad_total + term.astype(jnp.float32)
        in_grad = jnp.dot(hidden_rows.T, dinputs, preferred_element_type=jnp.float32)
        code_hot = (codes[:, step_id][:, None] == vocab[None, :]).astype(jnp.bfloat16)
        embed_grad = jnp.dot(code_hot.T, dinputs, preferred_element_type=jnp.float32)
        out_grad = jnp.dot(dlogits.T, normed, preferred_element_type=jnp.float32)
        ins.append(normalize(in_grad))
        embs.append(normalize(embed_grad))
        outs.append(normalize(out_grad))
        gains.append(normalize(gain_grad))
    return (grad_total.astype(jnp.bfloat16), jnp.stack(ins), jnp.stack(embs), jnp.stack(outs), jnp.stack(gains))
```

```python
import functools

import jax
import jax.numpy as jnp
import numpy as np
from jax import lax
from jax.experimental import pallas as pl
from jax.experimental.pallas import tpu as pltpu
from jax.sharding import PartitionSpec as P

F32, BF16 = jnp.float32, jnp.bfloat16
RING = 4
CONTRACT = (((0,), (0,)), ((), ()))


def dp_index(z, x, core):
    return (z * RING + x) * 2 + core


def way(core):
    return 1 - 2 * core


def dp_places():
    return [(z, x, c) for z in range(RING) for x in range(RING) for c in range(2)]


X_RING = [
    (dp_index(z, x, c), dp_index(z, (x + way(c)) % RING, c)) for z, x, c in dp_places()
]
Z_RING = [
    (dp_index(z, x, c), dp_index((z + way(c)) % RING, x, c)) for z, x, c in dp_places()
]
CORES = [(dp_index(z, x, c), dp_index(z, x, 1 - c)) for z, x, c in dp_places()]
Y_RING = [
    (y * 32 + dp_index(z, x, c), ((y + way(c)) % RING) * 32 + dp_index(z, x, c))
    for y in range(RING)
    for z, x, c in dp_places()
]


def shifts(axis, hop):
    pairs = []
    for z, x, c in dp_places():
        there = ((z + hop) % RING, x, c) if axis == "z" else (z, (x + hop) % RING, c)
        pairs.append((dp_index(z, x, c), dp_index(*there)))
    return pairs


def order(place, core):
    return [(place + (RING - 1 - k) * way(core)) % RING for k in range(RING)]


def tables(entries):
    rows = entries // 32
    vocab, head_blocks, in_blocks = [], [], []
    for z, x, c in dp_places():
        blocks = [
            dp_index(zz, xx, half)
            for half in (1 - c, c)
            for xx in order(x, half)
            for zz in order(z, half)
        ]
        head_blocks.append(blocks)
        vocab.append(np.concatenate([np.arange(b * rows, (b + 1) * rows) for b in blocks]))
        in_blocks.append([zz * RING + xx for zz in order(z, c) for xx in order(x, c)])
    return (
        np.array(vocab, np.int32),
        np.array(head_blocks, np.int32),
        np.array(in_blocks, np.int32),
    )


def reorder_kernel(blocks_ref, *refs):
    *sources, target = refs
    rows = sources[0].shape[0]
    for j, source in enumerate(sources):
        target[pl.ds(j * rows, rows)] = source[...]


def reorder(array, blocks):
    count, at_once = blocks.shape[0], 4
    rows, width = array.shape[0] // count, array.shape[1]

    def source_spec(j):
        return pl.BlockSpec((rows, width), lambda i, blocks_ref: (blocks_ref[at_once * i + j], 0))

    return pl.pallas_call(
        reorder_kernel,
        out_shape=jax.ShapeDtypeStruct(array.shape, array.dtype),
        grid_spec=pltpu.PrefetchScalarGridSpec(
            num_scalar_prefetch=1,
            grid=(count // at_once,),
            in_specs=[source_spec(j) for j in range(at_once)],
            out_specs=pl.BlockSpec((at_once * rows, width), lambda i, blocks_ref: (i, 0)),
        ),
        cost_estimate=pl.CostEstimate(
            flops=0, bytes_accessed=2 * array.size * array.dtype.itemsize, transcendentals=0
        ),
    )(blocks, *[array] * at_once)


def in_grad_kernel(blocks_ref, core_ref, r0, r1, r2, r3, d0, d1, d2, d3, other, own):
    left = jnp.concatenate([r0[...], r1[...], r2[...], r3[...]], axis=0)
    right = jnp.concatenate([d0[...], d1[...], d2[...], d3[...]], axis=0)
    both = lax.dot_general(left, right, CONTRACT, preferred_element_type=F32).astype(BF16)
    half = both.shape[0] // 2
    first = core_ref[0] == 0
    other[...] = jnp.where(first, both[half:], both[:half])
    own[...] = jnp.where(first, both[:half], both[half:])


def in_grad(blocks, core, rows, dinputs, part, parts):
    features = rows[0].shape[1]
    width = dinputs[0].shape[1] // parts
    count = 16
    pair = features // count
    frames = rows[0].shape[0]
    row_spec = pl.BlockSpec((frames, pair), lambda i, blocks_ref, core_ref: (0, blocks_ref[i]))
    d_spec = pl.BlockSpec((frames, width), lambda i, blocks_ref, core_ref: (0, part))
    own_spec = pl.BlockSpec((pair // 2, width), lambda i, blocks_ref, core_ref: (i, 0))

    def mirrored(k):
        return jnp.where(k < RING - 1, RING - 2 - k, k)

    other_spec = pl.BlockSpec(
        (pair // 2, width),
        lambda i, blocks_ref, core_ref: (mirrored(i // RING) * RING + mirrored(i % RING), 0),
    )
    out = jax.ShapeDtypeStruct((features // 2, width), BF16)
    return pl.pallas_call(
        in_grad_kernel,
        out_shape=(out, out),
        grid_spec=pltpu.PrefetchScalarGridSpec(
            num_scalar_prefetch=2,
            grid=(count,),
            in_specs=[row_spec] * 4 + [d_spec] * 4,
            out_specs=(other_spec, own_spec),
        ),
        compiler_params=pltpu.CompilerParams(vmem_limit_bytes=40 * 2**20),
        cost_estimate=pl.CostEstimate(
            flops=2 * 4 * frames * features * width,
            bytes_accessed=2 * 4 * frames * (features + width) + 2 * features * width,
            transcendentals=0,
        ),
    )(blocks, core, *rows, *dinputs)


def add(arrived, mine):
    return arrived.astype(F32) + mine.astype(F32)


def ring_scatter(chunks, send):
    part = chunks[0]
    for chunk in chunks[1:]:
        part = add(send(part), chunk).astype(BF16)
    return part


def direct_scatter(chunks, axis):
    core_first = lax.rem(lax.axis_index("dp"), 2) == 0
    up1 = jnp.where(core_first, chunks[2], chunks[0])
    up3 = jnp.where(core_first, chunks[0], chunks[2])
    total = chunks[3].astype(F32)
    for hop, chunk in ((1, up1), (3, up3), (2, chunks[1])):
        total = total + lax.ppermute(chunk, "dp", shifts(axis, hop)).astype(F32)
    return total


def squares(grad):
    return jnp.sum(grad * grad)


def per_device(hidden_rows, codes, targets, loss_weights, w_in, embed, w_out, gain):
    weight_in, table, head = w_in[0], embed[0], w_out[0]
    scale_gain = gain[0].astype(F32)
    entries, width = head.shape
    features = weight_in.shape[0]
    frames = hidden_rows.shape[0]
    y, dp = lax.axis_index("step"), lax.axis_index("dp")
    vocab_table, head_table, in_table = tables(entries)
    vocab = lax.dynamic_slice_in_dim(jnp.asarray(vocab_table), dp, 1, 0)
    head_blocks = lax.dynamic_slice_in_dim(jnp.asarray(head_table), dp, 1, 0)[0]
    in_blocks = lax.dynamic_slice_in_dim(jnp.asarray(in_table), dp, 1, 0)[0]
    core = lax.rem(dp, 2)
    step_way = 1 - 2 * core

    send_y = functools.partial(lax.ppermute, axis_name=("step", "dp"), perm=Y_RING)
    send_x = functools.partial(lax.ppermute, axis_name="dp", perm=X_RING)
    send_z = functools.partial(lax.ppermute, axis_name="dp", perm=Z_RING)
    swap = functools.partial(lax.ppermute, axis_name="dp", perm=CORES)

    half = frames // 2
    halves = [hidden_rows[:half], hidden_rows[half:]]
    blocks = [hidden_rows]
    for _ in range(RING - 1):
        halves = [send_y(piece) for piece in halves]
        blocks.append(jnp.concatenate(halves, axis=0))

    head = reorder(head, head_blocks)

    def of_block(array, k):
        owner = lax.rem(y + RING - k * step_way, RING)
        return lax.dynamic_slice_in_dim(array, owner * frames, frames, 0)

    normed, dlogits, dinputs, gains, terms, code_hots = [], [], [], [], [], []
    for k, rows in enumerate(blocks):
        code_col, target_col = of_block(codes, k), of_block(targets, k)
        weights = of_block(loss_weights, k)
        inputs = jnp.dot(rows, weight_in, preferred_element_type=F32)
        inputs = inputs + jnp.take(table, code_col[:, 0], axis=0).astype(F32)
        inverse = lax.rsqrt(jnp.mean(inputs * inputs, axis=-1, keepdims=True) + 1e-05)
        norm = (inputs * inverse * scale_gain).astype(BF16)
        logits = lax.dot_general(norm, head, (((1,), (1,)), ((), ())), preferred_element_type=F32)
        probs = jax.nn.softmax(logits, axis=-1)
        target_hot = (target_col == vocab).astype(F32)
        dlogit = (weights * (probs - target_hot)).astype(BF16)
        dnormed = jnp.dot(dlogit, head, preferred_element_type=F32)
        gains.append(jnp.sum(dnormed * inputs * inverse, axis=0))
        upstream = dnormed * scale_gain
        dinput = inverse * upstream - inputs * inverse**3 * jnp.mean(
            upstream * inputs, axis=-1, keepdims=True
        )
        dinput = dinput.astype(BF16)
        terms.append(
            lax.dot_general(
                dinput, weight_in, (((1,), (1,)), ((), ())), preferred_element_type=F32
            ).astype(BF16)
        )
        normed.append(norm)
        dlogits.append(dlogit)
        dinputs.append(dinput)
        code_hots.append((code_col == vocab).astype(BF16))

    row_part = ring_scatter([terms[1], terms[2], terms[3], terms[0]], send_y)

    def halves_of(left, right):
        left, right = jnp.concatenate(left, axis=0), jnp.concatenate(right, axis=0)
        middle = left.shape[1] // 2
        return [
            lax.dot_general(part, right, CONTRACT, preferred_element_type=F32)
            for part in (left[:, :middle], left[:, middle:])
        ]

    def cut(array, n):
        size = array.shape[0] // n
        return [array[i * size : (i + 1) * size] for i in range(n)]

    head_other, head_own = halves_of(dlogits, normed)
    head_sum = add(swap(head_other.astype(BF16)), head_own).astype(BF16)
    embed_other, embed_own = halves_of(code_hots, dinputs)
    embed_sum = add(swap(embed_other.astype(BF16)), embed_own).astype(BF16)
    gain_term = sum(gains).reshape(32, width // 32)
    gain_ring = jnp.take(gain_term, head_blocks, axis=0).astype(BF16)
    gain_sum = add(swap(gain_ring[:16]), gain_ring[16:]).astype(BF16)
    gain_chunks = [
        jnp.pad(chunk.reshape(1, 4 * width // 32), ((0, 15), (0, width - 4 * width // 32)))
        for chunk in cut(gain_sum, RING)
    ]
    head_line = ring_scatter(
        [jnp.concatenate(pair, axis=0) for pair in zip(cut(head_sum, RING), gain_chunks)], send_x
    )
    embed_line = ring_scatter(cut(embed_sum, RING), send_x)
    gain_line = head_line[-16:][0, : 4 * width // 32].reshape(RING, width // 32)
    head_line = head_line[:-16]
    small = [
        jnp.pad(gain_line[k : k + 1], ((0, 15), (0, width - width // 32))) for k in range(RING)
    ]
    mixed = direct_scatter(
        [
            jnp.concatenate(trio, axis=0)
            for trio in zip(cut(head_line, RING), cut(embed_line, RING), small)
        ],
        "z",
    )
    own_rows = entries // 32
    head_part, embed_part = mixed[:own_rows], mixed[own_rows : 2 * own_rows]
    gain_part = mixed[2 * own_rows, : width // 32]

    lines = []
    for part in range(2):
        other, own = in_grad(in_blocks, core[None], blocks, dinputs, part, 2)
        total = add(swap(other), own).astype(BF16)
        lines.append(ring_scatter(cut(total, RING), send_z))
    input_part = direct_scatter(
        [jnp.concatenate(pair, axis=1) for pair in zip(*(cut(line, RING) for line in lines))], "x"
    )

    sums = jnp.stack([squares(input_part), squares(embed_part), squares(head_part), squares(gain_part)])
    sums = lax.all_to_all(jnp.broadcast_to(sums, (32, 4)), "dp", 0, 0, tiled=True).sum(axis=0)
    sizes = jnp.array([features * width, entries * width, entries * width, width], F32)
    scales = lax.rsqrt(sums / sizes + 1e-06)
    return (
        row_part,
        (input_part * scales[0])[None],
        (embed_part * scales[1])[None],
        (head_part * scales[2])[None],
        (gain_part * scales[3])[None],
    )


def solution(mesh):
    in_specs = (
        P(("dp", "step"), None),
        P("dp", "step"),
        P("dp", "step"),
        P("dp", "step"),
        P("step", None, None),
        P("step", None, None),
        P("step", None, None),
        P("step", None),
    )
    out_specs = (
        P(("dp", "step"), None),
        P("step", "dp", None),
        P("step", "dp", None),
        P("step", "dp", None),
        P("step", "dp"),
    )
    return jax.shard_map(
        per_device, mesh=mesh, in_specs=in_specs, out_specs=out_specs, check_vma=False
    )
```

```python
import functools

import jax
import jax.numpy as jnp
import numpy as np
from jax import lax
from jax.experimental import pallas as pl
from jax.experimental.pallas import tpu as pltpu
from jax.sharding import PartitionSpec as P

F32, BF16 = jnp.float32, jnp.bfloat16
RING = 4
CONTRACT = (((0,), (0,)), ((), ()))


def dp_index(z, x, core):
    return (z * RING + x) * 2 + core


def way(core):
    return 1 - 2 * core


def dp_places():
    return [(z, x, c) for z in range(RING) for x in range(RING) for c in range(2)]


CORES = [(dp_index(z, x, c), dp_index(z, x, 1 - c)) for z, x, c in dp_places()]
Y_RING = [
    (y * 32 + dp_index(z, x, c), ((y + way(c)) % RING) * 32 + dp_index(z, x, c))
    for y in range(RING)
    for z, x, c in dp_places()
]
Y_BACK = [(there, here) for here, there in Y_RING]


def shifts(axis, hop):
    pairs = []
    for z, x, c in dp_places():
        there = ((z + hop) % RING, x, c) if axis == "z" else (z, (x + hop) % RING, c)
        pairs.append((dp_index(z, x, c), dp_index(*there)))
    return pairs


HOPS = (1, 2, 3, 0)


def order(place):
    return [(place + hop) % RING for hop in HOPS]


def tables(entries):
    rows = entries // 32
    vocab, head_blocks, in_blocks = [], [], []
    for z, x, c in dp_places():
        blocks = [
            dp_index(zz, xx, half) for half in (1 - c, c) for xx in order(x) for zz in order(z)
        ]
        head_blocks.append(blocks)
        vocab.append(np.concatenate([np.arange(b * rows, (b + 1) * rows) for b in blocks]))
        in_blocks.append(
            [dp_index(zz, xx, half) for half in (1 - c, c) for zz in order(z) for xx in order(x)]
        )
    return (
        np.array(vocab, np.int32),
        np.array(head_blocks, np.int32),
        np.array(in_blocks, np.int32),
    )


VMEM_LIMIT = 56 * 2**20
W_PARTS = 4


def whole(shape):
    return pl.BlockSpec(shape, lambda *_: (0,) * len(shape))


def block_kernel(
    n_rows, n_terms, first, places, columns, *refs
):
    rows_refs, refs = refs[:n_rows], refs[n_rows:]
    table_rows, target, weights, vocab, gain, w_in_hbm, head_hbm, *refs = refs
    if not first:
        gain_before, *refs = refs
        refs = refs[4:]
    normed_ref, dlogits_ref, dinputs_ref, ordered_ref, gain_ref, *refs = refs
    term_refs, refs = refs[:n_terms], refs[n_terms:]
    w_in, head, inputs_ref, rows, in_sem, head_sem = refs
    entries, width = head.shape
    features = w_in.shape[0]
    depth, piece, lanes = features // W_PARTS, entries // 32, features // 32

    in_copies = [
        pltpu.make_async_copy(
            w_in_hbm.at[pl.ds(i * depth, depth)], w_in.at[pl.ds(i * depth, depth)], in_sem.at[i]
        )
        for i in range(W_PARTS)
    ]
    head_copies = [
        pltpu.make_async_copy(
            head_hbm.at[pl.ds(places[i] * piece, piece)],
            head.at[pl.ds(i * piece, piece)],
            head_sem.at[i],
        )
        for i in range(32)
    ]
    for copy in in_copies + head_copies:
        copy.start()

    size = rows_refs[0].shape[0]
    for i, ref in enumerate(rows_refs):
        rows[i * size : (i + 1) * size] = ref[...]
    for i in range(32):
        ordered_ref[:, i * lanes : (i + 1) * lanes] = rows[
            :, pl.ds(pl.multiple_of(columns[i] * lanes, lanes), lanes)
        ]
    inputs_ref[...] = table_rows[...].astype(F32)
    for i, copy in enumerate(in_copies):
        copy.wait()
        inputs_ref[...] += jnp.dot(
            rows[:, i * depth : (i + 1) * depth],
            w_in[i * depth : (i + 1) * depth, :],
            preferred_element_type=F32,
        )
    inputs = inputs_ref[...]
    scale_gain = gain[...].astype(F32)
    inverse = lax.rsqrt(jnp.mean(inputs * inputs, axis=-1, keepdims=True) + 1e-05)
    normed = (inputs * inverse * scale_gain).astype(BF16)
    normed_ref[...] = normed
    for copy in head_copies:
        copy.wait()
    logits = lax.dot_general(
        normed, head[...], (((1,), (1,)), ((), ())), preferred_element_type=F32
    )
    powers = jnp.exp(logits - jnp.max(logits, axis=-1, keepdims=True))
    probs = powers * (1.0 / jnp.sum(powers, axis=-1, keepdims=True))
    target_hot = (target[...] == vocab[...]).astype(F32)
    dlogits = (weights[...] * (probs - target_hot)).astype(BF16)
    dlogits_ref[...] = dlogits
    dnormed = jnp.dot(dlogits, head[...], preferred_element_type=F32)
    inputs = inputs_ref[...]
    gain_term = jnp.sum(dnormed * inputs * inverse, axis=0, keepdims=True)
    gain_ref[...] = gain_term if first else gain_term + gain_before[...]
    upstream = dnormed * scale_gain
    dinputs = inverse * upstream - inputs * (
        inverse * inverse * inverse * jnp.mean(upstream * inputs, axis=-1, keepdims=True)
    )
    dinputs = dinputs.astype(BF16)
    dinputs_ref[...] = dinputs
    for j, term_ref in enumerate(term_refs):
        size = term_ref.shape[0]
        for i in range(W_PARTS):
            term_ref[:, i * depth : (i + 1) * depth] = lax.dot_general(
                dinputs[j * size : (j + 1) * size],
                w_in[i * depth : (i + 1) * depth, :],
                (((1,), (1,)), ((), ())),
                preferred_element_type=F32,
            ).astype(BF16)


def work_on_rows(
    at, places, columns, rows, table_rows, target, weights, vocab, gain, w_in, head, before, n_terms
):
    features, width = w_in.shape
    entries, count = head.shape[0], target.shape[0]
    frames = sum(piece.shape[0] for piece in rows)
    first = before is None

    def part(size):
        return pl.BlockSpec((frames, size), lambda *_: (at // frames, 0))

    hbm = pl.BlockSpec(memory_space=pl.ANY)
    shapes = [(width, BF16), (entries, BF16), (width, BF16), (features, BF16)]
    out_shape = [jax.ShapeDtypeStruct((count, n), t) for n, t in shapes]
    out_specs = [part(n) for n, _ in shapes]
    out_shape.append(jax.ShapeDtypeStruct((1, width), F32))
    out_specs.append(whole((1, width)))
    for _ in range(n_terms):
        out_shape.append(jax.ShapeDtypeStruct(rows[0].shape, BF16))
        out_specs.append(whole(rows[0].shape))
    operands = [*rows, table_rows, target, weights, vocab, gain, w_in, head]
    in_specs = [whole(piece.shape) for piece in rows] + [
        part(width), part(1), part(1), whole(vocab.shape), whole(gain.shape), hbm, hbm
    ]
    aliases = {}
    if not first:
        operands += [before[4], *before[:4]]
        in_specs += [whole((1, width))] + [hbm] * 4
        aliases = {2 + len(rows) + 8 + i: i for i in range(4)}
    return pl.pallas_call(
        functools.partial(block_kernel, len(rows), n_terms, first),
        out_shape=tuple(out_shape),
        grid_spec=pltpu.PrefetchScalarGridSpec(
            num_scalar_prefetch=2,
            grid=(1,),
            in_specs=in_specs,
            out_specs=tuple(out_specs),
            scratch_shapes=[
                pltpu.VMEM(w_in.shape, BF16),
                pltpu.VMEM(head.shape, BF16),
                pltpu.VMEM((frames, width), F32),
                pltpu.VMEM((frames, features), BF16),
                pltpu.SemaphoreType.DMA((W_PARTS,)),
                pltpu.SemaphoreType.DMA((32,)),
            ],
        ),
        input_output_aliases=aliases,
        compiler_params=pltpu.CompilerParams(vmem_limit_bytes=VMEM_LIMIT),
        cost_estimate=pl.CostEstimate(
            flops=4 * frames * width * (2 * features + 2 * entries),
            bytes_accessed=2 * (features * width + entries * width + 4 * frames * features),
            transcendentals=frames * entries,
        ),
    )(places, columns, *operands)


def cut(array, n):
    size = array.shape[0] // n
    return [array[i * size : (i + 1) * size] for i in range(n)]


def total(*terms):
    return sum(term.astype(F32) for term in terms)


def hop_by(axis, hop):
    return functools.partial(lax.ppermute, axis_name="dp", perm=shifts(axis, hop))


def direct_scatter(chunks, axis):
    arrived = [hop_by(axis, hop)(chunk) for hop, chunk in zip(HOPS, chunks[:-1])]
    return total(chunks[-1], *arrived)


def after(value, *others):
    return lax.optimization_barrier((value, others))[0]


class Ring:
    def __init__(self, one, two, axis):
        self.one, self.two = one, two
        self.up, self.down = hop_by(axis, 1), hop_by(axis, 3)

    def load(self):
        self.split = self.one[0][0].shape[0], self.two[0][0].shape[0]
        up = jnp.concatenate([total(*self.two[0]), total(*self.one[1])], axis=0)
        down = jnp.concatenate([total(*self.one[2]), total(*self.two[1])], axis=0)
        self.sent = up.astype(BF16), down.astype(BF16)
        return self.sent

    def first(self):
        self.below, self.above = self.up(self.sent[0]), self.down(self.sent[1])

    def second(self, *others):
        below, above = after((self.below, self.above), *others)
        self.two_below, above_rest = below[: self.split[1]], above[self.split[0] :]
        self.one_above, below_rest = above[: self.split[0]], below[self.split[1] :]
        self.sent = (
            total(below_rest, *self.one[0]).astype(BF16),
            total(above_rest, *self.two[2]).astype(BF16),
        )
        self.below, self.above = self.up(self.sent[0]), self.down(self.sent[1])
        return self.sent

    def result(self, *others):
        below, above = after((self.below, self.above), *others)
        return (
            total(below, self.one_above, *self.one[3]).astype(BF16),
            total(above, self.two_below, *self.two[3]).astype(BF16),
        )


def turn_kernel(source, target):
    target[...] = source[...].T


def turn(array):
    return pl.pallas_call(
        turn_kernel,
        out_shape=jax.ShapeDtypeStruct(array.shape[::-1], array.dtype),
        cost_estimate=pl.CostEstimate(
            flops=0, bytes_accessed=2 * array.size * array.dtype.itemsize, transcendentals=0
        ),
    )(array)


def squares(grad):
    return jnp.sum(grad * grad)


def per_device(hidden_rows, codes, targets, loss_weights, w_in, embed, w_out, gain):
    weight_in, table, head = w_in[0], embed[0], w_out[0]
    entries, width = head.shape
    features = weight_in.shape[0]
    frames = hidden_rows.shape[0]
    y, dp = lax.axis_index("step"), lax.axis_index("dp")
    vocab_table, head_table, in_table = tables(entries)
    vocab = lax.dynamic_slice_in_dim(jnp.asarray(vocab_table), dp, 1, 0)
    head_blocks = lax.dynamic_slice_in_dim(jnp.asarray(head_table), dp, 1, 0)[0]
    in_blocks = lax.dynamic_slice_in_dim(jnp.asarray(in_table), dp, 1, 0)[0]
    core = lax.rem(dp, 2)
    step_way = 1 - 2 * core

    send_y = functools.partial(lax.ppermute, axis_name=("step", "dp"), perm=Y_RING)
    swap = functools.partial(lax.ppermute, axis_name="dp", perm=CORES)

    back_y = functools.partial(lax.ppermute, axis_name=("step", "dp"), perm=Y_BACK)
    near = [send_y(hidden_rows), back_y(hidden_rows)]
    half = frames // 2
    far = [send_y(near[0][:half]), back_y(near[1][half:])]

    owners = lax.rem(y + RING + jnp.stack([-step_way, step_way, 0, 2]), RING)
    chosen = owners[:, None, None] == jnp.arange(RING)[None, :, None]

    def arranged(column):
        parts = column.reshape(1, RING, frames)
        return jnp.sum(jnp.where(chosen, parts, 0), axis=1)

    code_parts = arranged(codes)
    code_row = code_parts.reshape(1, RING * frames)
    code_col = code_parts.reshape(RING * frames, 1)
    target_col = arranged(targets).reshape(RING * frames, 1)
    weight_col = arranged(loss_weights).reshape(RING * frames, 1)
    ids = lax.broadcasted_iota(jnp.int32, (1, entries), 1)
    table_rows = jnp.dot(
        (code_col == ids).astype(BF16), table, preferred_element_type=F32
    ).astype(BF16)

    work = functools.partial(work_on_rows, places=head_blocks, columns=in_blocks)
    shared = dict(
        table_rows=table_rows, target=target_col, weights=weight_col, vocab=vocab, gain=gain,
        w_in=weight_in, head=head,
    )
    before = work(2 * frames, rows=[hidden_rows], before=None, n_terms=1, **shared)
    own_term = before[5]
    before = work(0, rows=near, before=before, n_terms=1, **shared)
    behind_term = before[5]
    before = work(3 * frames, rows=far, before=before, n_terms=0, **shared)
    normed, dlogits, dinputs, ordered, gain_term = before

    def row_term(place, left):
        return lax.dot_general(
            left[place * frames : (place + 1) * frames],
            weight_in,
            (((1,), (1,)), ((), ())),
            preferred_element_type=F32,
        )

    def product(left, right):
        return lax.dot_general(left, right, CONTRACT, preferred_element_type=F32).astype(BF16)

    def columns(array, n):
        size = array.shape[1] // n
        return [array[:, i * size : (i + 1) * size] for i in range(n)]

    def head_grad(half, left):
        return product(columns(left, 2)[half], normed)

    def embed_grad(half, right):
        hot = (vocab.reshape(2, entries // 2, 1)[half] == code_row).astype(BF16)
        return jnp.dot(hot, right, preferred_element_type=F32).astype(BF16)

    def in_grad(half, left):
        return product(left, columns(ordered, 2)[half])

    row_in = send_y(behind_term)
    in_other = in_grad(0, dinputs)
    head_other = head_grad(0, after(dlogits, in_other))
    embed_other = embed_grad(0, after(dinputs, head_other))
    in_own = in_grad(1, after(dinputs, embed_other))
    in_other, head_other, embed_other = swap(in_other), swap(head_other), swap(embed_other)
    in_chunks = [
        tuple(zip(*(cut(term, 2) for term in terms)))
        for terms in zip(columns(in_other, RING), columns(in_own, RING))
    ]
    in_ring = Ring([c[0] for c in in_chunks], [c[1] for c in in_chunks], "z")
    in_load = in_ring.load()
    in_ring.first()
    head_own = head_grad(1, after(dlogits, in_load))
    embed_own = embed_grad(1, after(dinputs, head_own))
    out_ring = Ring(
        list(zip(cut(head_other, RING), cut(head_own, RING))),
        list(zip(cut(embed_other, RING), cut(embed_own, RING))),
        "x",
    )
    out_load = out_ring.load()
    out_ring.first()
    row_sum = total(after(row_in, out_load), row_term(3, after(dinputs, out_load))).astype(BF16)
    row_in = send_y(row_sum)
    in_sent = in_ring.second(row_sum)
    out_sent = out_ring.second(in_sent)
    row_sum = total(after(row_in, out_sent), row_term(1, after(dinputs, out_sent))).astype(BF16)
    row_in = send_y(row_sum)
    in_line = jnp.concatenate(in_ring.result(row_sum), axis=0)
    input_part = direct_scatter(columns(in_line, RING), "x")
    out_line = out_ring.result(in_line)
    mixed = direct_scatter(
        [jnp.concatenate(pair, axis=0) for pair in zip(*(cut(line, RING) for line in out_line))],
        "z",
    )
    row_part = total(row_in, own_term).astype(BF16)
    own_rows = entries // 32
    head_part, embed_part = mixed[:own_rows], mixed[own_rows:]

    turned = turn(input_part)
    lane = lax.broadcasted_iota(jnp.int32, (32, 128), 1)
    sums = jnp.zeros((32, 128), F32)
    for i, grad in enumerate((input_part, embed_part, head_part)):
        sums = jnp.where(lane == i, squares(grad), sums)
    sums = jnp.concatenate([sums, jnp.broadcast_to(gain_term, (32, width))], axis=1)
    sums = lax.all_to_all(sums, "dp", 0, 0, tiled=True)
    sums = after(sums, turned, row_part).sum(axis=0)
    sums, gain_all = sums[:128], sums[128:]
    sizes = np.ones(128, np.float32)
    sizes[:3] = features * width, entries * width, entries * width
    scales = lax.rsqrt(sums / sizes + 1e-06)
    gain_part = lax.dynamic_slice_in_dim(gain_all, dp * (width // 32), width // 32, 0)
    gain_scale = lax.rsqrt(squares(gain_all) / width + 1e-06)
    return (
        row_part,
        (turned * scales[0])[None],
        (embed_part * scales[1])[None],
        (head_part * scales[2])[None],
        (gain_part * gain_scale)[None],
    )


def solution(mesh):
    in_specs = (
        P(("dp", "step"), None),
        P("dp", "step"),
        P("dp", "step"),
        P("dp", "step"),
        P("step", None, None),
        P("step", None, None),
        P("step", None, None),
        P("step", None),
    )
    out_specs = (
        P(("dp", "step"), None),
        P("step", "dp", None),
        P("step", "dp", None),
        P("step", "dp", None),
        P("step", "dp"),
    )
    return jax.shard_map(
        per_device, mesh=mesh, in_specs=in_specs, out_specs=out_specs, check_vma=False
    )
```

```python
import functools

import jax
import jax.numpy as jnp
import numpy as np
from jax import lax
from jax.experimental import pallas as pl
from jax.experimental.pallas import tpu as pltpu
from jax.sharding import PartitionSpec as P

F32, BF16 = jnp.float32, jnp.bfloat16
RING = 4
CONTRACT = (((0,), (0,)), ((), ()))


def dp_index(z, x, core):
    return (z * RING + x) * 2 + core


def way(core):
    return 1 - 2 * core


def dp_places():
    return [(z, x, c) for z in range(RING) for x in range(RING) for c in range(2)]


CORES = [(dp_index(z, x, c), dp_index(z, x, 1 - c)) for z, x, c in dp_places()]
Y_RING = [
    (y * 32 + dp_index(z, x, c), ((y + way(c)) % RING) * 32 + dp_index(z, x, c))
    for y in range(RING)
    for z, x, c in dp_places()
]
Y_BACK = [(there, here) for here, there in Y_RING]


def shifts(axis, hop):
    pairs = []
    for z, x, c in dp_places():
        there = ((z + hop) % RING, x, c) if axis == "z" else (z, (x + hop) % RING, c)
        pairs.append((dp_index(z, x, c), dp_index(*there)))
    return pairs


HOPS = (1, 2, 3, 0)
HEAD_HOPS = (2, 3, 1, 0)
EMBED_HOPS = (1, 2, 3, 0)
LOW, HIGH = (1, 2), (3, 0)
IN_HOPS = ((1, HIGH), (2, LOW), (2, HIGH), (3, LOW), (1, LOW), (3, HIGH), (0, LOW), (0, HIGH))


def tables(entries):
    rows = entries // 32
    head_blocks, embed_blocks, in_blocks = [], [], []
    for z, x, c in dp_places():
        for blocks, hops in ((head_blocks, HEAD_HOPS), (embed_blocks, EMBED_HOPS)):
            blocks.append(
                [
                    dp_index((z + dz) % RING, (x + dx) % RING, half)
                    for half in (1 - c, c)
                    for dx in hops
                    for dz in HOPS
                ]
            )
        in_blocks.append(
            [
                dp_index((z + dz) % RING, (x + dx) % RING, half)
                for half in (1 - c, c)
                for dz, part in IN_HOPS
                for dx in part
            ]
        )
    head_blocks, embed_blocks, in_blocks = (
        np.array(blocks, np.int32) for blocks in (head_blocks, embed_blocks, in_blocks)
    )
    entry = np.arange(rows, dtype=np.int32)
    head_vocab, embed_vocab = (
        (blocks[:, :, None] * rows + entry).reshape(32, entries)
        for blocks in (head_blocks, embed_blocks)
    )
    return head_blocks, head_vocab, embed_vocab, in_blocks


VMEM_LIMIT = 56 * 2**20
W_PARTS = 8
AHEAD = 4


def whole(shape):
    return pl.BlockSpec(shape, lambda *_: (0,) * len(shape))


def block_kernel(
    n_rows, n_terms, first, places, columns, *refs
):
    rows_refs, refs = refs[:n_rows], refs[n_rows:]
    table_rows, target, weights, vocab, gain, w_in_hbm, head_hbm, *refs = refs
    if not first:
        gain_before, *refs = refs
        refs = refs[4:]
    normed_ref, dlogits_ref, dinputs_ref, ordered_ref, gain_ref, *refs = refs
    term_refs, refs = refs[:n_terms], refs[n_terms:]
    w_in, head, inputs_ref, rows, in_sem, head_sem = refs
    entries, width = head.shape
    features = w_in.shape[0]
    depth, piece, lanes = features // W_PARTS, entries // 32, features // 32

    in_copies = [
        pltpu.make_async_copy(
            w_in_hbm.at[pl.ds(i * depth, depth)], w_in.at[pl.ds(i * depth, depth)], in_sem.at[i]
        )
        for i in range(W_PARTS)
    ]
    head_copies = [
        pltpu.make_async_copy(
            head_hbm.at[pl.ds(places[i] * piece, piece)],
            head.at[pl.ds(i * piece, piece)],
            head_sem.at[i],
        )
        for i in range(32)
    ]
    size = rows_refs[0].shape[0]
    waiting = [[copy] for copy in in_copies] + [head_copies[i : i + 8] for i in range(0, 32, 8)]

    def start_next():
        for copy in waiting.pop(0):
            copy.start()

    for _ in range(AHEAD):
        start_next()

    inputs_ref[...] = table_rows[...].astype(F32)
    for i, ref in enumerate(rows_refs):
        rows[i * size : (i + 1) * size] = ref[...]
    for i in range(32):
        ordered_ref[:, i * lanes : (i + 1) * lanes] = rows[
            :, pl.ds(pl.multiple_of(columns[i] * lanes, lanes), lanes)
        ]
    for i, copy in enumerate(in_copies):
        copy.wait()
        if waiting:
            start_next()
        inputs_ref[...] += jnp.dot(
            rows[:, i * depth : (i + 1) * depth],
            w_in[i * depth : (i + 1) * depth, :],
            preferred_element_type=F32,
        )
    while waiting:
        start_next()
    inputs = inputs_ref[...]
    scale_gain = gain[...].astype(F32)
    inverse = lax.rsqrt(jnp.mean(inputs * inputs, axis=-1, keepdims=True) + 1e-05)
    normed = (inputs * inverse * scale_gain).astype(BF16)
    normed_ref[...] = normed
    for copy in head_copies:
        copy.wait()
    logits = lax.dot_general(
        normed, head[...], (((1,), (1,)), ((), ())), preferred_element_type=F32
    )
    powers = jnp.exp(logits - jnp.max(logits, axis=-1, keepdims=True))
    probs = powers * (1.0 / jnp.sum(powers, axis=-1, keepdims=True))
    target_hot = (target[...] == vocab[...]).astype(F32)
    dlogits = (weights[...] * (probs - target_hot)).astype(BF16)
    dlogits_ref[...] = dlogits
    dnormed = jnp.dot(dlogits, head[...], preferred_element_type=F32)
    inputs = inputs_ref[...]
    gain_term = jnp.sum(dnormed * inputs * inverse, axis=0, keepdims=True)
    gain_ref[...] = gain_term if first else gain_term + gain_before[...]
    upstream = dnormed * scale_gain
    dinputs = inverse * upstream - inputs * (
        inverse * inverse * inverse * jnp.mean(upstream * inputs, axis=-1, keepdims=True)
    )
    dinputs = dinputs.astype(BF16)
    dinputs_ref[...] = dinputs
    for j, term_ref in enumerate(term_refs):
        size = term_ref.shape[0]
        for i in range(W_PARTS):
            term_ref[:, i * depth : (i + 1) * depth] = lax.dot_general(
                dinputs[j * size : (j + 1) * size],
                w_in[i * depth : (i + 1) * depth, :],
                (((1,), (1,)), ((), ())),
                preferred_element_type=F32,
            ).astype(BF16)


def work_on_rows(
    at, places, columns, rows, table_rows, target, weights, vocab, gain, w_in, head, before, n_terms
):
    features, width = w_in.shape
    entries, count = head.shape[0], target.shape[0]
    frames = sum(piece.shape[0] for piece in rows)
    first = before is None

    def part(size):
        return pl.BlockSpec((frames, size), lambda *_: (at // frames, 0))

    hbm = pl.BlockSpec(memory_space=pl.ANY)
    shapes = [(width, BF16), (entries, BF16), (width, BF16), (features, BF16)]
    out_shape = [jax.ShapeDtypeStruct((count, n), t) for n, t in shapes]
    out_specs = [part(n) for n, _ in shapes]
    out_shape.append(jax.ShapeDtypeStruct((1, width), F32))
    out_specs.append(whole((1, width)))
    for _ in range(n_terms):
        out_shape.append(jax.ShapeDtypeStruct(rows[0].shape, BF16))
        out_specs.append(whole(rows[0].shape))
    operands = [*rows, table_rows, target, weights, vocab, gain, w_in, head]
    in_specs = [whole(piece.shape) for piece in rows] + [
        part(width), part(1), part(1), whole(vocab.shape), whole(gain.shape), hbm, hbm
    ]
    aliases = {}
    if not first:
        operands += [before[4], *before[:4]]
        in_specs += [whole((1, width))] + [hbm] * 4
        aliases = {2 + len(rows) + 8 + i: i for i in range(4)}
    return pl.pallas_call(
        functools.partial(block_kernel, len(rows), n_terms, first),
        out_shape=tuple(out_shape),
        grid_spec=pltpu.PrefetchScalarGridSpec(
            num_scalar_prefetch=2,
            grid=(1,),
            in_specs=in_specs,
            out_specs=tuple(out_specs),
            scratch_shapes=[
                pltpu.VMEM(w_in.shape, BF16),
                pltpu.VMEM(head.shape, BF16),
                pltpu.VMEM((frames, width), F32),
                pltpu.VMEM((frames, features), BF16),
                pltpu.SemaphoreType.DMA((W_PARTS,)),
                pltpu.SemaphoreType.DMA((32,)),
            ],
        ),
        input_output_aliases=aliases,
        compiler_params=pltpu.CompilerParams(vmem_limit_bytes=VMEM_LIMIT),
        cost_estimate=pl.CostEstimate(
            flops=4 * frames * width * (2 * features + 2 * entries),
            bytes_accessed=2 * (features * width + entries * width + 4 * frames * features),
            transcendentals=frames * entries,
        ),
    )(places, columns, *operands)


def cut(array, n):
    size = array.shape[0] // n
    return [array[i * size : (i + 1) * size] for i in range(n)]


def total(*terms):
    return sum(term.astype(F32) for term in terms)


def hop_by(axis, hop):
    return functools.partial(lax.ppermute, axis_name="dp", perm=shifts(axis, hop))


def direct_scatter(chunks, axis):
    arrived = [hop_by(axis, hop)(chunk) for hop, chunk in zip(HOPS, chunks[:-1])]
    return total(chunks[-1], *arrived)


def after(value, *others):
    return lax.optimization_barrier((value, others))[0]


def turn_kernel(source, target):
    target[...] = source[...].T


def turn(array):
    return pl.pallas_call(
        turn_kernel,
        out_shape=jax.ShapeDtypeStruct(array.shape[::-1], array.dtype),
        cost_estimate=pl.CostEstimate(flops=0, bytes_accessed=array.size, transcendentals=0),
    )(array)


def finish_kernel(n_in, n_table, payload, turned, mixed, upd_in, upd_embed, upd_out, upd_gain):
    sums = jnp.sum(payload[...], axis=0, keepdims=True)
    size = upd_gain.shape[1]

    def scale(place, count):
        return lax.rsqrt(sums[:, place : place + 1] / count + 1e-06)

    half = upd_out.shape[0]
    upd_in[...] = turned[...] * scale(0, n_in)
    upd_embed[...] = mixed[half:] * scale(1, n_table)
    upd_out[...] = mixed[:half] * scale(2, n_table)
    gain = sums[:, 128:]
    mean = jnp.mean(gain * gain, axis=1, keepdims=True)
    upd_gain[...] = sums[:, size : 2 * size] * lax.rsqrt(mean + 1e-06)


def finish(payload, turned, mixed):
    rows, width = mixed.shape
    shapes = [turned.shape, (rows // 2, width), (rows // 2, width), (1, width // 32)]
    return pl.pallas_call(
        functools.partial(finish_kernel, 32 * turned.size, 16 * mixed.size),
        out_shape=tuple(jax.ShapeDtypeStruct(shape, F32) for shape in shapes),
        cost_estimate=pl.CostEstimate(
            flops=2 * turned.size, bytes_accessed=16 * turned.size, transcendentals=0
        ),
    )(payload, turned, mixed)


def squares(grad):
    return jnp.sum(grad * grad)


def per_device(hidden_rows, codes, targets, loss_weights, w_in, embed, w_out, gain):
    weight_in, table, head = w_in[0], embed[0], w_out[0]
    entries, width = head.shape
    features = weight_in.shape[0]
    frames = hidden_rows.shape[0]
    y, dp = lax.axis_index("step"), lax.axis_index("dp")
    head_blocks, vocab, embed_vocab, in_blocks = (
        lax.dynamic_slice_in_dim(jnp.asarray(table), dp, 1, 0) for table in tables(entries)
    )
    head_blocks, in_blocks = head_blocks[0], in_blocks[0]
    core = lax.rem(dp, 2)
    step_way = 1 - 2 * core

    send_y = functools.partial(lax.ppermute, axis_name=("step", "dp"), perm=Y_RING)
    swap = functools.partial(lax.ppermute, axis_name="dp", perm=CORES)

    back_y = functools.partial(lax.ppermute, axis_name=("step", "dp"), perm=Y_BACK)
    near = [send_y(hidden_rows), back_y(hidden_rows)]
    half = frames // 2
    far = [send_y(near[0][:half]), back_y(near[1][half:])]

    owners = lax.rem(y + RING + jnp.stack([-step_way, step_way, 0, 2]), RING)
    chosen = owners[:, None, None] == jnp.arange(RING)[None, :, None]

    def arranged(column):
        parts = column.reshape(1, RING, frames)
        return jnp.sum(jnp.where(chosen, parts, 0), axis=1)

    code_parts = arranged(codes)
    code_row = code_parts.reshape(1, RING * frames)
    code_col = code_parts.reshape(RING * frames, 1)
    target_col = arranged(targets).reshape(RING * frames, 1)
    weight_col = arranged(loss_weights).reshape(RING * frames, 1)
    ids = lax.broadcasted_iota(jnp.int32, (1, entries), 1)
    table_rows = jnp.dot(
        (code_col == ids).astype(BF16), table, preferred_element_type=F32
    ).astype(BF16)

    work = functools.partial(work_on_rows, places=head_blocks, columns=in_blocks)
    shared = dict(
        table_rows=table_rows, target=target_col, weights=weight_col, vocab=vocab, gain=gain,
        w_in=weight_in, head=head,
    )
    before = work(2 * frames, rows=[hidden_rows], before=None, n_terms=1, **shared)
    own_term = before[5]
    before = work(0, rows=near, before=before, n_terms=1, **shared)
    behind_term = before[5]
    before = work(3 * frames, rows=far, before=before, n_terms=0, **shared)
    normed, dlogits, dinputs, ordered, gain_term = before

    def row_term(place, left):
        return lax.dot_general(
            left[place * frames : (place + 1) * frames],
            weight_in,
            (((1,), (1,)), ((), ())),
            preferred_element_type=F32,
        )

    def product(left, right):
        return lax.dot_general(left, right, CONTRACT, preferred_element_type=F32).astype(BF16)

    def columns(array, n):
        size = array.shape[1] // n
        return [array[:, i * size : (i + 1) * size] for i in range(n)]

    def head_grad(half, part, left):
        return product(columns(left, 4)[2 * half + part], normed)

    def embed_grad(half, part, right):
        ids = embed_vocab.reshape(4, entries // 4, 1)[2 * half + part]
        return jnp.dot((ids == code_row).astype(BF16), right, preferred_element_type=F32).astype(BF16)

    def in_grad(half, part, left):
        return product(left, columns(ordered, 4)[2 * half + part])

    up_x, down_x, up_z, down_z = (hop_by(axis, hop) for axis in "xz" for hop in (1, 3))

    row_in = send_y(behind_term)
    in_other = in_grad(0, 0, dinputs)
    head_other = head_grad(0, 0, after(dlogits, in_other))
    embed_other = embed_grad(0, 0, after(dinputs, head_other))
    in_own = in_grad(1, 0, after(dinputs, embed_other))
    in_other, head_other, embed_other = swap(in_other), swap(head_other), swap(embed_other)
    in_load = [total(*terms).astype(BF16) for terms in zip(columns(in_other, 2), columns(in_own, 2))]
    in_below, in_above = up_z(in_load[0]), down_z(in_load[1])
    head_own = head_grad(1, 0, after(dlogits, in_load))
    embed_own = embed_grad(1, 0, after(dinputs, head_own))
    head_far, head_down = (total(*terms) for terms in zip(cut(head_other, 2), cut(head_own, 2)))
    embed_up, embed_far = (total(*terms) for terms in zip(cut(embed_other, 2), cut(embed_own, 2)))
    out_load = [
        jnp.concatenate(pair, axis=0).astype(BF16)
        for pair in ((embed_up, head_far), (head_down, embed_far))
    ]
    out_below, out_above = up_x(out_load[0]), down_x(out_load[1])

    in_other = in_grad(0, 1, after(dinputs, out_load, row_in))
    in_own = in_grad(1, 1, after(dinputs, in_other))
    row_sum = total(row_in, row_term(3, after(dinputs, in_own))).astype(BF16)
    row_in = send_y(row_sum)
    head_other = head_grad(0, 1, after(dlogits, row_sum))
    head_own = head_grad(1, 1, after(dlogits, head_other))
    embed_other = embed_grad(0, 1, after(dinputs, head_own))
    embed_own = embed_grad(1, 1, after(dinputs, embed_other))
    in_other, head_other, embed_other = swap(in_other), swap(head_other), swap(embed_other)
    in_rest = list(zip(columns(in_other, 4), columns(in_own, 4)))
    head_rest = list(zip(cut(head_other, 2), cut(head_own, 2)))
    embed_rest = list(zip(cut(embed_other, 2), cut(embed_own, 2)))
    ahead_term = after(row_term(1, after(dinputs, embed_own)).astype(BF16))

    in_below, in_above = after((in_below, in_above), ahead_term)
    (in_two, below), (above, in_one) = columns(in_below, 2), columns(in_above, 2)
    in_sent = total(below, *in_rest[0]).astype(BF16), total(above, *in_rest[1]).astype(BF16)
    in_below, in_above = up_z(in_sent[0]), down_z(in_sent[1])
    out_below, out_above = after((out_below, out_above), in_sent)
    (out_two, below), (out_one, above) = cut(out_below, 2), cut(out_above, 2)
    out_sent = total(below, *head_rest[0]).astype(BF16), total(above, *embed_rest[0]).astype(BF16)
    out_below, out_above = up_x(out_sent[0]), down_x(out_sent[1])

    in_below, in_above = after((in_below, in_above), out_sent)
    in_low = total(in_below, in_one, *in_rest[2]).astype(BF16)
    in_high = total(in_above, in_two, *in_rest[3]).astype(BF16)
    input_part = direct_scatter(columns(in_low, 2) + columns(in_high, 2), "x")
    out_below, out_above = after((out_below, out_above), in_low, in_high)
    head_line = total(out_below, out_one, *head_rest[1]).astype(BF16)
    embed_line = total(out_above, out_two, *embed_rest[1]).astype(BF16)
    mixed = direct_scatter(
        [jnp.concatenate(pair, axis=0) for pair in zip(cut(head_line, RING), cut(embed_line, RING))],
        "z",
    )
    row_sum = total(after(row_in, mixed, input_part), ahead_term).astype(BF16)
    row_part = total(send_y(row_sum), own_term).astype(BF16)
    own_rows = entries // 32
    head_part, embed_part = mixed[:own_rows], mixed[own_rows:]

    turned = turn(input_part)
    lane = lax.broadcasted_iota(jnp.int32, (32, 32), 1)
    sums = jnp.zeros((32, 32), F32)
    for i, grad in enumerate((input_part, embed_part, head_part)):
        sums = jnp.where(lane == i, squares(grad), sums)
    gain_parts = after(gain_term).reshape(32, width // 32)
    payload = jnp.concatenate(
        [sums, gain_parts, jnp.zeros((32, 64), F32), jnp.broadcast_to(gain_term, (32, width))],
        axis=1,
    )
    payload = lax.all_to_all(payload, "dp", 0, 0, tiled=True)
    upd_in, upd_embed, upd_out, upd_gain = finish(after(payload, turned, row_part), turned, mixed)
    return row_part, upd_in[None], upd_embed[None], upd_out[None], upd_gain


def solution(mesh):
    in_specs = (
        P(("dp", "step"), None),
        P("dp", "step"),
        P("dp", "step"),
        P("dp", "step"),
        P("step", None, None),
        P("step", None, None),
        P("step", None, None),
        P("step", None),
    )
    out_specs = (
        P(("dp", "step"), None),
        P("step", "dp", None),
        P("step", "dp", None),
        P("step", "dp", None),
        P("step", "dp"),
    )
    return jax.shard_map(
        per_device, mesh=mesh, in_specs=in_specs, out_specs=out_specs, check_vma=False
    )
```

```python
import functools

import jax
import jax.numpy as jnp
import numpy as np
from jax import lax
from jax.experimental import pallas as pl
from jax.experimental.pallas import tpu as pltpu
from jax.sharding import PartitionSpec as P

F32, BF16 = jnp.float32, jnp.bfloat16
RING = 4
CONTRACT = (((0,), (0,)), ((), ()))


def dp_index(z, x, core):
    return (z * RING + x) * 2 + core


def way(core):
    return 1 - 2 * core


def dp_places():
    return [(z, x, c) for z in range(RING) for x in range(RING) for c in range(2)]


CORES = [(dp_index(z, x, c), dp_index(z, x, 1 - c)) for z, x, c in dp_places()]
Y_RING = [
    (y * 32 + dp_index(z, x, c), ((y + way(c)) % RING) * 32 + dp_index(z, x, c))
    for y in range(RING)
    for z, x, c in dp_places()
]
Y_BACK = [(there, here) for here, there in Y_RING]


def shifts(axis, hop):
    pairs = []
    for z, x, c in dp_places():
        there = ((z + hop) % RING, x, c) if axis == "z" else (z, (x + hop) % RING, c)
        pairs.append((dp_index(z, x, c), dp_index(*there)))
    return pairs


HOPS = (1, 2, 3, 0)
HEAD_HOPS = (2, 3, 1, 0)
EMBED_HOPS = (1, 2, 3, 0)
LOW, HIGH = (1, 2), (3, 0)
IN_HOPS = ((1, HIGH), (2, LOW), (2, HIGH), (3, LOW), (1, LOW), (3, HIGH), (0, LOW), (0, HIGH))


def tables(entries):
    rows = entries // 32
    head_blocks, embed_blocks, in_blocks = [], [], []
    for z, x, c in dp_places():
        for blocks, hops in ((head_blocks, HEAD_HOPS), (embed_blocks, EMBED_HOPS)):
            blocks.append(
                [
                    dp_index((z + dz) % RING, (x + dx) % RING, half)
                    for half in (1 - c, c)
                    for dx in hops
                    for dz in HOPS
                ]
            )
        in_blocks.append(
            [
                dp_index((z + dz) % RING, (x + dx) % RING, half)
                for half in (1 - c, c)
                for dz, part in IN_HOPS
                for dx in part
            ]
        )
    head_blocks, embed_blocks, in_blocks = (
        np.array(blocks, np.int32) for blocks in (head_blocks, embed_blocks, in_blocks)
    )
    entry = np.arange(rows, dtype=np.int32)
    head_vocab, embed_vocab = (
        (blocks[:, :, None] * rows + entry).reshape(32, entries)
        for blocks in (head_blocks, embed_blocks)
    )
    return head_blocks, head_vocab, embed_vocab, in_blocks


VMEM_LIMIT = 56 * 2**20
W_PARTS = 8
AHEAD = 4


def whole(shape):
    return pl.BlockSpec(shape, lambda *_: (0,) * len(shape))


def block_kernel(
    n_rows, n_terms, first, places, columns, *refs
):
    rows_refs, refs = refs[:n_rows], refs[n_rows:]
    table_rows, target, weights, vocab, gain, w_in_hbm, head_hbm, *refs = refs
    if not first:
        gain_before, *refs = refs
        refs = refs[4:]
    normed_ref, dlogits_ref, dinputs_ref, ordered_ref, gain_ref, *refs = refs
    term_refs, refs = refs[:n_terms], refs[n_terms:]
    w_in, head, inputs_ref, rows, in_sem, head_sem = refs
    entries, width = head.shape
    features = w_in.shape[0]
    depth, piece, lanes = features // W_PARTS, entries // 32, features // 32

    in_copies = [
        pltpu.make_async_copy(
            w_in_hbm.at[pl.ds(i * depth, depth)], w_in.at[pl.ds(i * depth, depth)], in_sem.at[i]
        )
        for i in range(W_PARTS)
    ]
    head_copies = [
        pltpu.make_async_copy(
            head_hbm.at[pl.ds(places[i] * piece, piece)],
            head.at[pl.ds(i * piece, piece)],
            head_sem.at[i],
        )
        for i in range(32)
    ]
    size = rows_refs[0].shape[0]
    waiting = [[copy] for copy in in_copies] + [head_copies[i : i + 8] for i in range(0, 32, 8)]

    def start_next():
        for copy in waiting.pop(0):
            copy.start()

    for _ in range(AHEAD):
        start_next()

    inputs_ref[...] = table_rows[...].astype(F32)
    for i, ref in enumerate(rows_refs):
        rows[i * size : (i + 1) * size] = ref[...]
    for i in range(32):
        ordered_ref[:, i * lanes : (i + 1) * lanes] = rows[
            :, pl.ds(pl.multiple_of(columns[i] * lanes, lanes), lanes)
        ]
    for i, copy in enumerate(in_copies):
        copy.wait()
        if waiting:
            start_next()
        inputs_ref[...] += jnp.dot(
            rows[:, i * depth : (i + 1) * depth],
            w_in[i * depth : (i + 1) * depth, :],
            preferred_element_type=F32,
        )
    while waiting:
        start_next()
    inputs = inputs_ref[...]
    scale_gain = gain[...].astype(F32)
    inverse = lax.rsqrt(jnp.mean(inputs * inputs, axis=-1, keepdims=True) + 1e-05)
    normed = (inputs * inverse * scale_gain).astype(BF16)
    normed_ref[...] = normed
    for copy in head_copies:
        copy.wait()
    logits = lax.dot_general(
        normed, head[...], (((1,), (1,)), ((), ())), preferred_element_type=F32
    )
    powers = jnp.exp(logits - jnp.max(logits, axis=-1, keepdims=True))
    probs = powers * (1.0 / jnp.sum(powers, axis=-1, keepdims=True))
    target_hot = (target[...] == vocab[...]).astype(F32)
    dlogits = (weights[...] * (probs - target_hot)).astype(BF16)
    dlogits_ref[...] = dlogits
    dnormed = jnp.dot(dlogits, head[...], preferred_element_type=F32)
    inputs = inputs_ref[...]
    gain_term = jnp.sum(dnormed * inputs * inverse, axis=0, keepdims=True)
    gain_ref[...] = gain_term if first else gain_term + gain_before[...]
    upstream = dnormed * scale_gain
    dinputs = inverse * upstream - inputs * (
        inverse * inverse * inverse * jnp.mean(upstream * inputs, axis=-1, keepdims=True)
    )
    dinputs = dinputs.astype(BF16)
    dinputs_ref[...] = dinputs
    for j, term_ref in enumerate(term_refs):
        size = term_ref.shape[0]
        for i in range(W_PARTS):
            term_ref[:, i * depth : (i + 1) * depth] = lax.dot_general(
                dinputs[j * size : (j + 1) * size],
                w_in[i * depth : (i + 1) * depth, :],
                (((1,), (1,)), ((), ())),
                preferred_element_type=F32,
            ).astype(BF16)


def work_on_rows(
    at, places, columns, rows, table_rows, target, weights, vocab, gain, w_in, head, before, n_terms
):
    features, width = w_in.shape
    entries, count = head.shape[0], target.shape[0]
    frames = sum(piece.shape[0] for piece in rows)
    first = before is None

    def part(size):
        return pl.BlockSpec((frames, size), lambda *_: (at // frames, 0))

    hbm = pl.BlockSpec(memory_space=pl.ANY)
    shapes = [(width, BF16), (entries, BF16), (width, BF16), (features, BF16)]
    out_shape = [jax.ShapeDtypeStruct((count, n), t) for n, t in shapes]
    out_specs = [part(n) for n, _ in shapes]
    out_shape.append(jax.ShapeDtypeStruct((1, width), F32))
    out_specs.append(whole((1, width)))
    for _ in range(n_terms):
        out_shape.append(jax.ShapeDtypeStruct(rows[0].shape, BF16))
        out_specs.append(whole(rows[0].shape))
    operands = [*rows, table_rows, target, weights, vocab, gain, w_in, head]
    in_specs = [whole(piece.shape) for piece in rows] + [
        part(width), part(1), part(1), whole(vocab.shape), whole(gain.shape), hbm, hbm
    ]
    aliases = {}
    if not first:
        operands += [before[4], *before[:4]]
        in_specs += [whole((1, width))] + [hbm] * 4
        aliases = {2 + len(rows) + 8 + i: i for i in range(4)}
    return pl.pallas_call(
        functools.partial(block_kernel, len(rows), n_terms, first),
        out_shape=tuple(out_shape),
        grid_spec=pltpu.PrefetchScalarGridSpec(
            num_scalar_prefetch=2,
            grid=(1,),
            in_specs=in_specs,
            out_specs=tuple(out_specs),
            scratch_shapes=[
                pltpu.VMEM(w_in.shape, BF16),
                pltpu.VMEM(head.shape, BF16),
                pltpu.VMEM((frames, width), F32),
                pltpu.VMEM((frames, features), BF16),
                pltpu.SemaphoreType.DMA((W_PARTS,)),
                pltpu.SemaphoreType.DMA((32,)),
            ],
        ),
        input_output_aliases=aliases,
        compiler_params=pltpu.CompilerParams(vmem_limit_bytes=VMEM_LIMIT),
        cost_estimate=pl.CostEstimate(
            flops=4 * frames * width * (2 * features + 2 * entries),
            bytes_accessed=2 * (features * width + entries * width + 4 * frames * features),
            transcendentals=frames * entries,
        ),
    )(places, columns, *operands)


def cut(array, n):
    size = array.shape[0] // n
    return [array[i * size : (i + 1) * size] for i in range(n)]


def total(*terms):
    return sum(term.astype(F32) for term in terms)


def hop_by(axis, hop):
    return functools.partial(lax.ppermute, axis_name="dp", perm=shifts(axis, hop))


def direct_scatter(chunks, axis):
    arrived = [hop_by(axis, hop)(chunk) for hop, chunk in zip(HOPS, chunks[:-1])]
    return total(chunks[-1], *arrived)


def after(value, *others):
    return lax.optimization_barrier((value, others))[0]


def turn_kernel(source, target):
    target[...] = source[...].T


def turn(array):
    return pl.pallas_call(
        turn_kernel,
        out_shape=jax.ShapeDtypeStruct(array.shape[::-1], array.dtype),
        cost_estimate=pl.CostEstimate(flops=0, bytes_accessed=array.size, transcendentals=0),
    )(array)


def finish_kernel(n_in, n_table, payload, turned, mixed, upd_in, upd_embed, upd_out, upd_gain):
    sums = jnp.sum(payload[...], axis=0, keepdims=True)
    size = upd_gain.shape[1]

    def scale(place, count):
        return lax.rsqrt(sums[:, place : place + 1] / count + 1e-06)

    half = upd_out.shape[0]
    upd_in[...] = turned[...] * scale(0, n_in)
    upd_embed[...] = mixed[half:] * scale(1, n_table)
    upd_out[...] = mixed[:half] * scale(2, n_table)
    gain = sums[:, 128:]
    mean = jnp.mean(gain * gain, axis=1, keepdims=True)
    upd_gain[...] = sums[:, size : 2 * size] * lax.rsqrt(mean + 1e-06)


def finish(payload, turned, mixed):
    rows, width = mixed.shape
    shapes = [turned.shape, (rows // 2, width), (rows // 2, width), (1, width // 32)]
    return pl.pallas_call(
        functools.partial(finish_kernel, 32 * turned.size, 16 * mixed.size),
        out_shape=tuple(jax.ShapeDtypeStruct(shape, F32) for shape in shapes),
        cost_estimate=pl.CostEstimate(
            flops=2 * turned.size, bytes_accessed=16 * turned.size, transcendentals=0
        ),
    )(payload, turned, mixed)


def squares(grad):
    return jnp.sum(grad * grad)


def per_device(hidden_rows, codes, targets, loss_weights, w_in, embed, w_out, gain):
    weight_in, table, head = w_in[0], embed[0], w_out[0]
    entries, width = head.shape
    features = weight_in.shape[0]
    frames = hidden_rows.shape[0]
    y, dp = lax.axis_index("step"), lax.axis_index("dp")
    head_blocks, vocab, embed_vocab, in_blocks = (
        lax.dynamic_slice_in_dim(jnp.asarray(table), dp, 1, 0) for table in tables(entries)
    )
    head_blocks, in_blocks = head_blocks[0], in_blocks[0]
    core = lax.rem(dp, 2)
    step_way = 1 - 2 * core

    send_y = functools.partial(lax.ppermute, axis_name=("step", "dp"), perm=Y_RING)
    swap = functools.partial(lax.ppermute, axis_name="dp", perm=CORES)

    back_y = functools.partial(lax.ppermute, axis_name=("step", "dp"), perm=Y_BACK)
    near = [send_y(hidden_rows), back_y(hidden_rows)]
    half = frames // 2
    far = [send_y(near[0][:half]), back_y(near[1][half:])]

    owners = lax.rem(y + RING + jnp.stack([-step_way, step_way, 0, 2]), RING)
    chosen = owners[:, None, None] == jnp.arange(RING)[None, :, None]

    def arranged(column):
        parts = column.reshape(1, RING, frames)
        return jnp.sum(jnp.where(chosen, parts, 0), axis=1)

    code_parts = arranged(codes)
    code_row = code_parts.reshape(1, RING * frames)
    code_col = code_parts.reshape(RING * frames, 1)
    target_col = arranged(targets).reshape(RING * frames, 1)
    weight_col = arranged(loss_weights).reshape(RING * frames, 1)
    ids = lax.broadcasted_iota(jnp.int32, (1, entries), 1)
    table_rows = jnp.dot(
        (code_col == ids).astype(BF16), table, preferred_element_type=F32
    ).astype(BF16)

    work = functools.partial(work_on_rows, places=head_blocks, columns=in_blocks)
    shared = dict(
        table_rows=table_rows, target=target_col, weights=weight_col, vocab=vocab, gain=gain,
        w_in=weight_in, head=head,
    )
    before = work(2 * frames, rows=[hidden_rows], before=None, n_terms=1, **shared)
    own_term = before[5]
    before = work(0, rows=near, before=before, n_terms=1, **shared)
    behind_term = before[5]
    before = work(3 * frames, rows=far, before=before, n_terms=0, **shared)
    normed, dlogits, dinputs, ordered, gain_term = before

    def row_term(place, left):
        return lax.dot_general(
            left[place * frames : (place + 1) * frames],
            weight_in,
            (((1,), (1,)), ((), ())),
            preferred_element_type=F32,
        )

    def product(left, right):
        return lax.dot_general(left, right, CONTRACT, preferred_element_type=F32).astype(BF16)

    def columns(array, n):
        size = array.shape[1] // n
        return [array[:, i * size : (i + 1) * size] for i in range(n)]

    def head_grad(half, part, left):
        return product(columns(left, 4)[2 * half + part], normed)

    def embed_grad(half, part, right):
        ids = embed_vocab.reshape(4, entries // 4, 1)[2 * half + part]
        return jnp.dot((ids == code_row).astype(BF16), right, preferred_element_type=F32).astype(BF16)

    def in_grad(half, part, left):
        return product(left, columns(ordered, 4)[2 * half + part])

    up_x, down_x, up_z, down_z = (hop_by(axis, hop) for axis in "xz" for hop in (1, 3))

    row_in = send_y(behind_term)
    in_other = in_grad(0, 0, dinputs)
    head_other = head_grad(0, 0, after(dlogits, in_other))
    embed_other = embed_grad(0, 0, after(dinputs, head_other))
    in_own = in_grad(1, 0, after(dinputs, embed_other))
    in_other, head_other, embed_other = swap(in_other), swap(head_other), swap(embed_other)
    in_load = [total(*terms).astype(BF16) for terms in zip(columns(in_other, 2), columns(in_own, 2))]
    in_below, in_above = up_z(in_load[0]), down_z(in_load[1])
    head_own = head_grad(1, 0, after(dlogits, in_load))
    embed_own = embed_grad(1, 0, after(dinputs, head_own))
    head_far, head_down = (total(*terms) for terms in zip(cut(head_other, 2), cut(head_own, 2)))
    embed_up, embed_far = (total(*terms) for terms in zip(cut(embed_other, 2), cut(embed_own, 2)))
    out_load = [
        jnp.concatenate(pair, axis=0).astype(BF16)
        for pair in ((embed_up, head_far), (head_down, embed_far))
    ]
    out_below, out_above = up_x(out_load[0]), down_x(out_load[1])

    in_other = in_grad(0, 1, after(dinputs, out_load))
    in_own = in_grad(1, 1, after(dinputs, in_other, row_in))
    row_sum = total(row_in, row_term(3, after(dinputs, in_own))).astype(BF16)
    row_in = send_y(row_sum)
    head_other = head_grad(0, 1, after(dlogits, row_sum))
    head_own = head_grad(1, 1, after(dlogits, head_other))
    embed_other = embed_grad(0, 1, after(dinputs, head_own))
    embed_own = embed_grad(1, 1, after(dinputs, embed_other))
    in_other, head_other, embed_other = swap(in_other), swap(head_other), swap(embed_other)
    in_rest = list(zip(columns(in_other, 4), columns(in_own, 4)))
    head_rest = list(zip(cut(head_other, 2), cut(head_own, 2)))
    embed_rest = list(zip(cut(embed_other, 2), cut(embed_own, 2)))

    in_below, in_above = after((in_below, in_above), embed_own)
    (in_two, below), (above, in_one) = columns(in_below, 2), columns(in_above, 2)
    in_sent = total(below, *in_rest[0]).astype(BF16), total(above, *in_rest[1]).astype(BF16)
    in_below, in_above = up_z(in_sent[0]), down_z(in_sent[1])
    out_below, out_above = after((out_below, out_above), in_sent)
    (out_two, below), (out_one, above) = cut(out_below, 2), cut(out_above, 2)
    out_sent = total(below, *head_rest[0]).astype(BF16), total(above, *embed_rest[0]).astype(BF16)
    out_below, out_above = up_x(out_sent[0]), down_x(out_sent[1])
    ahead_term = after(row_term(1, after(dinputs, out_sent)).astype(BF16))

    gain_parts = after(gain_term).reshape(32, width // 32)
    gain_side = jnp.concatenate(
        [gain_parts, jnp.zeros((32, 64), F32), jnp.broadcast_to(gain_term, (32, width))], axis=1
    )
    in_below, in_above = after((in_below, in_above), ahead_term, gain_side)
    in_low = total(in_below, in_one, *in_rest[2]).astype(BF16)
    in_high = total(in_above, in_two, *in_rest[3]).astype(BF16)
    input_part = direct_scatter(columns(in_low, 2) + columns(in_high, 2), "x")
    row_sum = total(after(row_in, in_low, in_high), ahead_term).astype(BF16)
    out_below, out_above = after((out_below, out_above), row_sum)
    head_line = total(out_below, out_one, *head_rest[1]).astype(BF16)
    embed_line = total(out_above, out_two, *embed_rest[1]).astype(BF16)
    mixed = direct_scatter(
        [jnp.concatenate(pair, axis=0) for pair in zip(cut(head_line, RING), cut(embed_line, RING))],
        "z",
    )
    row_part = total(send_y(after(row_sum, mixed, input_part)), own_term).astype(BF16)
    own_rows = entries // 32
    head_part, embed_part = mixed[:own_rows], mixed[own_rows:]

    turned = turn(input_part)
    lane = lax.broadcasted_iota(jnp.int32, (32, 32), 1)
    sums = jnp.zeros((32, 32), F32)
    for i, grad in enumerate((input_part, embed_part, head_part)):
        sums = jnp.where(lane == i, squares(grad), sums)
    payload = jnp.concatenate([sums, gain_side], axis=1)
    payload = lax.all_to_all(payload, "dp", 0, 0, tiled=True)
    upd_in, upd_embed, upd_out, upd_gain = finish(after(payload, turned, row_part), turned, mixed)
    return row_part, upd_in[None], upd_embed[None], upd_out[None], upd_gain


def solution(mesh):
    in_specs = (
        P(("dp", "step"), None),
        P("dp", "step"),
        P("dp", "step"),
        P("dp", "step"),
        P("step", None, None),
        P("step", None, None),
        P("step", None, None),
        P("step", None),
    )
    out_specs = (
        P(("dp", "step"), None),
        P("step", "dp", None),
        P("step", "dp", None),
        P("step", "dp", None),
        P("step", "dp"),
    )
    return jax.shard_map(
        per_device, mesh=mesh, in_specs=in_specs, out_specs=out_specs, check_vma=False
    )
```

```python
import functools

import jax
import jax.numpy as jnp
import numpy as np
from jax import lax
from jax.experimental import pallas as pl
from jax.experimental.pallas import tpu as pltpu
from jax.sharding import PartitionSpec as P

F32, BF16 = jnp.float32, jnp.bfloat16
RING = 4
CONTRACT = (((0,), (0,)), ((), ()))


def dp_index(z, x, core):
    return (z * RING + x) * 2 + core


def way(core):
    return 1 - 2 * core


def dp_places():
    return [(z, x, c) for z in range(RING) for x in range(RING) for c in range(2)]


CORES = [(dp_index(z, x, c), dp_index(z, x, 1 - c)) for z, x, c in dp_places()]
Y_RING = [
    (y * 32 + dp_index(z, x, c), ((y + way(c)) % RING) * 32 + dp_index(z, x, c))
    for y in range(RING)
    for z, x, c in dp_places()
]
Y_BACK = [(there, here) for here, there in Y_RING]


def shifts(axis, hop):
    pairs = []
    for z, x, c in dp_places():
        there = ((z + hop) % RING, x, c) if axis == "z" else (z, (x + hop) % RING, c)
        pairs.append((dp_index(z, x, c), dp_index(*there)))
    return pairs


HOPS = (1, 2, 3, 0)
HEAD_HOPS = (2, 3, 1, 0)
EMBED_HOPS = (1, 2, 3, 0)
LOW, HIGH = (1, 2), (3, 0)
IN_HOPS = ((1, HIGH), (2, LOW), (2, HIGH), (3, LOW), (1, LOW), (3, HIGH), (0, LOW), (0, HIGH))


def tables(entries):
    rows = entries // 32
    head_blocks, embed_blocks, in_blocks = [], [], []
    for z, x, c in dp_places():
        for blocks, hops in ((head_blocks, HEAD_HOPS), (embed_blocks, EMBED_HOPS)):
            blocks.append(
                [
                    dp_index((z + dz) % RING, (x + dx) % RING, half)
                    for half in (1 - c, c)
                    for dx in hops
                    for dz in HOPS
                ]
            )
        in_blocks.append(
            [
                dp_index((z + dz) % RING, (x + dx) % RING, half)
                for half in (1 - c, c)
                for dz, part in IN_HOPS
                for dx in part
            ]
        )
    head_blocks, embed_blocks, in_blocks = (
        np.array(blocks, np.int32) for blocks in (head_blocks, embed_blocks, in_blocks)
    )
    entry = np.arange(rows, dtype=np.int32)
    head_vocab, embed_vocab = (
        (blocks[:, :, None] * rows + entry).reshape(32, entries)
        for blocks in (head_blocks, embed_blocks)
    )
    return head_blocks, head_vocab, embed_vocab, in_blocks


VMEM_LIMIT = 56 * 2**20
W_PARTS = 8
AHEAD = 4


def whole(shape):
    return pl.BlockSpec(shape, lambda *_: (0,) * len(shape))


def block_kernel(
    n_rows, n_terms, first, places, columns, *refs
):
    rows_refs, refs = refs[:n_rows], refs[n_rows:]
    table_rows, target, weights, vocab, gain, w_in_hbm, head_hbm, *refs = refs
    if not first:
        gain_before, *refs = refs
        refs = refs[4:]
    normed_ref, dlogits_ref, dinputs_ref, ordered_ref, gain_ref, *refs = refs
    term_refs, refs = refs[:n_terms], refs[n_terms:]
    w_in, head, inputs_ref, rows, in_sem, head_sem = refs
    entries, width = head.shape
    features = w_in.shape[0]
    depth, piece, lanes = features // W_PARTS, entries // 32, features // 32

    in_copies = [
        pltpu.make_async_copy(
            w_in_hbm.at[pl.ds(i * depth, depth)], w_in.at[pl.ds(i * depth, depth)], in_sem.at[i]
        )
        for i in range(W_PARTS)
    ]
    head_copies = [
        pltpu.make_async_copy(
            head_hbm.at[pl.ds(places[i] * piece, piece)],
            head.at[pl.ds(i * piece, piece)],
            head_sem.at[i],
        )
        for i in range(32)
    ]
    size = rows_refs[0].shape[0]
    waiting = [[copy] for copy in in_copies] + [head_copies[i : i + 8] for i in range(0, 32, 8)]

    def start_next():
        for copy in waiting.pop(0):
            copy.start()

    for _ in range(AHEAD):
        start_next()

    inputs_ref[...] = table_rows[...].astype(F32)
    for i, ref in enumerate(rows_refs):
        rows[i * size : (i + 1) * size] = ref[...]
    for i in range(32):
        ordered_ref[:, i * lanes : (i + 1) * lanes] = rows[
            :, pl.ds(pl.multiple_of(columns[i] * lanes, lanes), lanes)
        ]
    for i, copy in enumerate(in_copies):
        copy.wait()
        if waiting:
            start_next()
        inputs_ref[...] += jnp.dot(
            rows[:, i * depth : (i + 1) * depth],
            w_in[i * depth : (i + 1) * depth, :],
            preferred_element_type=F32,
        )
    while waiting:
        start_next()
    inputs = inputs_ref[...]
    scale_gain = gain[...].astype(F32)
    inverse = lax.rsqrt(jnp.mean(inputs * inputs, axis=-1, keepdims=True) + 1e-05)
    normed = (inputs * inverse * scale_gain).astype(BF16)
    normed_ref[...] = normed
    for copy in head_copies:
        copy.wait()
    logits = lax.dot_general(
        normed, head[...], (((1,), (1,)), ((), ())), preferred_element_type=F32
    )
    powers = jnp.exp(logits - jnp.max(logits, axis=-1, keepdims=True))
    probs = powers * (1.0 / jnp.sum(powers, axis=-1, keepdims=True))
    target_hot = (target[...] == vocab[...]).astype(F32)
    dlogits = (weights[...] * (probs - target_hot)).astype(BF16)
    dlogits_ref[...] = dlogits
    dnormed = jnp.dot(dlogits, head[...], preferred_element_type=F32)
    inputs = inputs_ref[...]
    gain_term = jnp.sum(dnormed * inputs * inverse, axis=0, keepdims=True)
    gain_ref[...] = gain_term if first else gain_term + gain_before[...]
    upstream = dnormed * scale_gain
    dinputs = inverse * upstream - inputs * (
        inverse * inverse * inverse * jnp.mean(upstream * inputs, axis=-1, keepdims=True)
    )
    dinputs = dinputs.astype(BF16)
    dinputs_ref[...] = dinputs
    for j, term_ref in enumerate(term_refs):
        size = term_ref.shape[0]
        for i in range(W_PARTS):
            term_ref[:, i * depth : (i + 1) * depth] = lax.dot_general(
                dinputs[j * size : (j + 1) * size],
                w_in[i * depth : (i + 1) * depth, :],
                (((1,), (1,)), ((), ())),
                preferred_element_type=F32,
            ).astype(BF16)


def work_on_rows(
    at, places, columns, rows, table_rows, target, weights, vocab, gain, w_in, head, before, n_terms
):
    features, width = w_in.shape
    entries, count = head.shape[0], target.shape[0]
    frames = sum(piece.shape[0] for piece in rows)
    first = before is None

    def part(size):
        return pl.BlockSpec((frames, size), lambda *_: (at // frames, 0))

    hbm = pl.BlockSpec(memory_space=pl.ANY)
    shapes = [(width, BF16), (entries, BF16), (width, BF16), (features, BF16)]
    out_shape = [jax.ShapeDtypeStruct((count, n), t) for n, t in shapes]
    out_specs = [part(n) for n, _ in shapes]
    out_shape.append(jax.ShapeDtypeStruct((1, width), F32))
    out_specs.append(whole((1, width)))
    for _ in range(n_terms):
        out_shape.append(jax.ShapeDtypeStruct(rows[0].shape, BF16))
        out_specs.append(whole(rows[0].shape))
    operands = [*rows, table_rows, target, weights, vocab, gain, w_in, head]
    in_specs = [whole(piece.shape) for piece in rows] + [
        part(width), part(1), part(1), whole(vocab.shape), whole(gain.shape), hbm, hbm
    ]
    aliases = {}
    if not first:
        operands += [before[4], *before[:4]]
        in_specs += [whole((1, width))] + [hbm] * 4
        aliases = {2 + len(rows) + 8 + i: i for i in range(4)}
    return pl.pallas_call(
        functools.partial(block_kernel, len(rows), n_terms, first),
        out_shape=tuple(out_shape),
        grid_spec=pltpu.PrefetchScalarGridSpec(
            num_scalar_prefetch=2,
            grid=(1,),
            in_specs=in_specs,
            out_specs=tuple(out_specs),
            scratch_shapes=[
                pltpu.VMEM(w_in.shape, BF16),
                pltpu.VMEM(head.shape, BF16),
                pltpu.VMEM((frames, width), F32),
                pltpu.VMEM((frames, features), BF16),
                pltpu.SemaphoreType.DMA((W_PARTS,)),
                pltpu.SemaphoreType.DMA((32,)),
            ],
        ),
        input_output_aliases=aliases,
        compiler_params=pltpu.CompilerParams(vmem_limit_bytes=VMEM_LIMIT),
        cost_estimate=pl.CostEstimate(
            flops=4 * frames * width * (2 * features + 2 * entries),
            bytes_accessed=2 * (features * width + entries * width + 4 * frames * features),
            transcendentals=frames * entries,
        ),
    )(places, columns, *operands)


def cut(array, n):
    size = array.shape[0] // n
    return [array[i * size : (i + 1) * size] for i in range(n)]


def total(*terms):
    return sum(term.astype(F32) for term in terms)


def hop_by(axis, hop):
    return functools.partial(lax.ppermute, axis_name="dp", perm=shifts(axis, hop))


def direct_scatter(chunks, axis):
    arrived = [hop_by(axis, hop)(chunk) for hop, chunk in zip(HOPS, chunks[:-1])]
    return total(chunks[-1], *arrived)


def after(value, *others):
    return lax.optimization_barrier((value, others))[0]


def turn_kernel(source, target):
    target[...] = source[...].T


def turn(array):
    return pl.pallas_call(
        turn_kernel,
        out_shape=jax.ShapeDtypeStruct(array.shape[::-1], array.dtype),
        cost_estimate=pl.CostEstimate(flops=0, bytes_accessed=array.size, transcendentals=0),
    )(array)


def finish_kernel(n_in, n_table, payload, turned, mixed, upd_in, upd_embed, upd_out, upd_gain):
    sums = jnp.sum(payload[...], axis=0, keepdims=True)
    size = upd_gain.shape[1]

    def scale(place, count):
        return lax.rsqrt(sums[:, place : place + 1] / count + 1e-06)

    half = upd_out.shape[0]
    upd_in[...] = turned[...] * scale(0, n_in)
    upd_embed[...] = mixed[half:] * scale(1, n_table)
    upd_out[...] = mixed[:half] * scale(2, n_table)
    gain = sums[:, 128:]
    mean = jnp.mean(gain * gain, axis=1, keepdims=True)
    upd_gain[...] = sums[:, size : 2 * size] * lax.rsqrt(mean + 1e-06)


def finish(payload, turned, mixed):
    rows, width = mixed.shape
    shapes = [turned.shape, (rows // 2, width), (rows // 2, width), (1, width // 32)]
    return pl.pallas_call(
        functools.partial(finish_kernel, 32 * turned.size, 16 * mixed.size),
        out_shape=tuple(jax.ShapeDtypeStruct(shape, F32) for shape in shapes),
        cost_estimate=pl.CostEstimate(
            flops=2 * turned.size, bytes_accessed=16 * turned.size, transcendentals=0
        ),
    )(payload, turned, mixed)


def squares(grad):
    return jnp.sum(grad * grad)


def per_device(hidden_rows, codes, targets, loss_weights, w_in, embed, w_out, gain):
    weight_in, table, head = w_in[0], embed[0], w_out[0]
    entries, width = head.shape
    features = weight_in.shape[0]
    frames = hidden_rows.shape[0]
    y, dp = lax.axis_index("step"), lax.axis_index("dp")
    head_blocks, vocab, embed_vocab, in_blocks = (
        lax.dynamic_slice_in_dim(jnp.asarray(table), dp, 1, 0) for table in tables(entries)
    )
    head_blocks, in_blocks = head_blocks[0], in_blocks[0]
    core = lax.rem(dp, 2)
    step_way = 1 - 2 * core

    send_y = functools.partial(lax.ppermute, axis_name=("step", "dp"), perm=Y_RING)
    swap = functools.partial(lax.ppermute, axis_name="dp", perm=CORES)

    back_y = functools.partial(lax.ppermute, axis_name=("step", "dp"), perm=Y_BACK)
    near = [send_y(hidden_rows), back_y(hidden_rows)]
    half = frames // 2
    far = [send_y(near[0][:half]), back_y(near[1][half:])]

    owners = lax.rem(y + RING + jnp.stack([-step_way, step_way, 0, 2]), RING)
    chosen = owners[:, None, None] == jnp.arange(RING)[None, :, None]

    def arranged(column):
        parts = column.reshape(1, RING, frames)
        return jnp.sum(jnp.where(chosen, parts, 0), axis=1)

    code_parts = arranged(codes)
    code_row = code_parts.reshape(1, RING * frames)
    code_col = code_parts.reshape(RING * frames, 1)
    target_col = arranged(targets).reshape(RING * frames, 1)
    weight_col = arranged(loss_weights).reshape(RING * frames, 1)
    ids = lax.broadcasted_iota(jnp.int32, (1, entries), 1)
    table_rows = jnp.dot(
        (code_col == ids).astype(BF16), table, preferred_element_type=F32
    ).astype(BF16)

    work = functools.partial(work_on_rows, places=head_blocks, columns=in_blocks)
    shared = dict(
        table_rows=table_rows, target=target_col, weights=weight_col, vocab=vocab, gain=gain,
        w_in=weight_in, head=head,
    )
    before = work(2 * frames, rows=[hidden_rows], before=None, n_terms=1, **shared)
    own_term = before[5]
    before = work(0, rows=near, before=before, n_terms=1, **shared)
    behind_term = before[5]
    before = work(3 * frames, rows=far, before=before, n_terms=0, **shared)
    normed, dlogits, dinputs, ordered, gain_term = before

    def row_term(place, left):
        return lax.dot_general(
            left[place * frames : (place + 1) * frames],
            weight_in,
            (((1,), (1,)), ((), ())),
            preferred_element_type=F32,
        )

    def product(left, right):
        return lax.dot_general(left, right, CONTRACT, preferred_element_type=F32).astype(BF16)

    def columns(array, n):
        size = array.shape[1] // n
        return [array[:, i * size : (i + 1) * size] for i in range(n)]

    def head_grad(half, part, left):
        return product(columns(left, 4)[2 * half + part], normed)

    def embed_grad(half, part, right):
        ids = embed_vocab.reshape(4, entries // 4, 1)[2 * half + part]
        return jnp.dot((ids == code_row).astype(BF16), right, preferred_element_type=F32).astype(BF16)

    def in_grad(half, part, left):
        return product(left, columns(ordered, 4)[2 * half + part])

    up_x, down_x, up_z, down_z = (hop_by(axis, hop) for axis in "xz" for hop in (1, 3))

    row_in = send_y(behind_term)
    in_other = in_grad(0, 0, dinputs)
    head_other = head_grad(0, 0, after(dlogits, in_other))
    embed_other = embed_grad(0, 0, after(dinputs, head_other))
    in_own = in_grad(1, 0, after(dinputs, embed_other))
    in_other, head_other, embed_other = swap(in_other), swap(head_other), swap(embed_other)
    in_load = [total(*terms).astype(BF16) for terms in zip(columns(in_other, 2), columns(in_own, 2))]
    in_below, in_above = up_z(in_load[0]), down_z(in_load[1])
    head_own = head_grad(1, 0, after(dlogits, in_load))
    embed_own = embed_grad(1, 0, after(dinputs, head_own))
    head_far, head_down = (total(*terms) for terms in zip(cut(head_other, 2), cut(head_own, 2)))
    embed_up, embed_far = (total(*terms) for terms in zip(cut(embed_other, 2), cut(embed_own, 2)))
    out_load = [
        jnp.concatenate(pair, axis=0).astype(BF16)
        for pair in ((embed_up, head_far), (head_down, embed_far))
    ]
    out_below, out_above = up_x(out_load[0]), down_x(out_load[1])

    in_other = in_grad(0, 1, after(dinputs, out_load))
    in_own = in_grad(1, 1, after(dinputs, in_other, row_in))
    row_sum = total(row_in, row_term(3, after(dinputs, in_own))).astype(BF16)
    row_in = send_y(row_sum)
    head_other = head_grad(0, 1, after(dlogits, row_sum))
    head_own = head_grad(1, 1, after(dlogits, head_other))
    embed_other = embed_grad(0, 1, after(dinputs, head_own))
    embed_own = embed_grad(1, 1, after(dinputs, embed_other))
    in_other, head_other, embed_other = swap(in_other), swap(head_other), swap(embed_other)
    in_rest = list(zip(columns(in_other, 4), columns(in_own, 4)))
    head_rest = list(zip(cut(head_other, 2), cut(head_own, 2)))
    embed_rest = list(zip(cut(embed_other, 2), cut(embed_own, 2)))

    in_below, in_above = after((in_below, in_above), embed_own)
    (in_two, below), (above, in_one) = columns(in_below, 2), columns(in_above, 2)
    in_sent = total(below, *in_rest[0]).astype(BF16), total(above, *in_rest[1]).astype(BF16)
    in_below, in_above = up_z(in_sent[0]), down_z(in_sent[1])
    out_below, out_above = after((out_below, out_above), in_sent)
    (out_two, below), (out_one, above) = cut(out_below, 2), cut(out_above, 2)
    out_sent = total(below, *head_rest[0]).astype(BF16), total(above, *embed_rest[0]).astype(BF16)
    out_below, out_above = up_x(out_sent[0]), down_x(out_sent[1])
    ahead_term = after(row_term(1, after(dinputs, out_sent)).astype(BF16))

    gain_parts = after(gain_term).reshape(32, width // 32)
    gain_side = jnp.concatenate(
        [gain_parts, jnp.zeros((32, 64), F32), jnp.broadcast_to(gain_term, (32, width))], axis=1
    )
    gain_side = after(gain_side)
    in_below, in_above = after((in_below, in_above), ahead_term, gain_side)
    in_low = total(in_below, in_one, *in_rest[2]).astype(BF16)
    in_high = total(in_above, in_two, *in_rest[3]).astype(BF16)
    input_part = direct_scatter(columns(in_low, 2) + columns(in_high, 2), "x")
    row_sum = total(after(row_in, in_low, in_high), ahead_term).astype(BF16)
    out_below, out_above = after((out_below, out_above), row_sum)
    head_line = total(out_below, out_one, *head_rest[1]).astype(BF16)
    embed_line = total(out_above, out_two, *embed_rest[1]).astype(BF16)
    mixed = direct_scatter(
        [jnp.concatenate(pair, axis=0) for pair in zip(cut(head_line, RING), cut(embed_line, RING))],
        "z",
    )
    row_part = total(send_y(after(row_sum, mixed, input_part)), own_term).astype(BF16)
    own_rows = entries // 32
    head_part, embed_part = mixed[:own_rows], mixed[own_rows:]

    turned = turn(input_part)
    lane = lax.broadcasted_iota(jnp.int32, (32, 32), 1)
    sums = jnp.zeros((32, 32), F32)
    for i, grad in enumerate((input_part, embed_part, head_part)):
        sums = jnp.where(lane == i, squares(grad), sums)
    payload = jnp.concatenate([sums, gain_side], axis=1)
    payload = lax.all_to_all(payload, "dp", 0, 0, tiled=True)
    upd_in, upd_embed, upd_out, upd_gain = finish(after(payload, turned, row_part), turned, mixed)
    return row_part, upd_in[None], upd_embed[None], upd_out[None], upd_gain


def solution(mesh):
    in_specs = (
        P(("dp", "step"), None),
        P("dp", "step"),
        P("dp", "step"),
        P("dp", "step"),
        P("step", None, None),
        P("step", None, None),
        P("step", None, None),
        P("step", None),
    )
    out_specs = (
        P(("dp", "step"), None),
        P("step", "dp", None),
        P("step", "dp", None),
        P("step", "dp", None),
        P("step", "dp"),
    )
    return jax.shard_map(
        per_device, mesh=mesh, in_specs=in_specs, out_specs=out_specs, check_vma=False
    )
```
